32 devices in a mesh: seq: 16 (over z, x, core), row: 2 (over y).
Axes of the slice: x: 2, y: 2, z: 4, core: 2. Of those that a mesh axis runs over, the one named last changes fastest.
Arguments:
- queries: bfloat16 [2, 16, 128, 3072], P(None, 'seq', 'row'), may hold values from -9 to 9
- keys: bfloat16 [2, 16, 128, 512], P(None, 'seq', 'row'), may hold values from -9 to 9
- values: bfloat16 [2, 16, 128, 512], P(None, 'seq', 'row'), may hold values from -6 to 6
- gain: float32 [128], replicated, may hold values from 0.1 to 1.9
Outputs:
- attended: bfloat16 [2, 16, 128, 3072], P(None, 'seq', 'row')
The draws below stay inside these ranges and needn't reach their ends.
All inputs are finite; a program needn't handle non-finite values.
Results may differ from the reference program's by a relative error of at most 0.017.
Values may be sent and summed in bfloat16 or wider, within the bound.
A program may use at most 128 MiB of HBM per device.

```python
import math
import jax
import jax.numpy as jnp
from jax import lax

BLOCK = 128
KV_HEADS = 4
GROUP = 6
HEAD_DIM = 128
HEADS = 24
BLOCKS = 32
SEQ_LEN = 4096


def to_layout_drawn(sequence_rows):
    width_now = sequence_rows.shape[-1]
    blocked = sequence_rows.reshape(BLOCKS, BLOCK, width_now)
    half_count = BLOCKS // 2
    return jnp.stack([blocked[:half_count], blocked[half_count:][::-1]], axis=0)


def draw_queries(key, part):
    width_now = HEADS * HEAD_DIM
    drawn = jnp.clip(jax.random.normal(jax.random.fold_in(key, 11), (SEQ_LEN, width_now), jnp.float32), -6.0, 6.0)
    return to_layout_drawn(drawn).astype(jnp.bfloat16)


def draw_keys(key, part):
    width_now = KV_HEADS * HEAD_DIM
    drawn = jnp.clip(jax.random.normal(jax.random.fold_in(key, 13), (SEQ_LEN, width_now), jnp.float32), -6.0, 6.0)
    return to_layout_drawn(drawn).astype(jnp.bfloat16)


def block_scale(own_key, extent, split, low, top_value):
    loudness = 1.0
    for axis_at, shards_of in split:
        steps = jax.random.uniform(jax.random.fold_in(jax.random.fold_in(own_key, 6), axis_at), (shards_of,), jnp.float32, low / len(split), top_value / len(split))
        loudness = loudness * jnp.repeat(jnp.exp(steps), extent[axis_at] // shards_of).reshape((-1,) + (1,) * (len(extent) - 1 - axis_at))
    return loudness


def normal_values(stream_key, extent, scale, reach, shards=(), kind=jnp.bfloat16):
    factor_of = block_scale(stream_key, extent, shards, -0.22, 0.18) if shards else 1.0
    array = jax.random.normal(stream_key, extent, jnp.float32) * scale * factor_of
    return jnp.minimum(jnp.maximum(array, -reach), reach).astype(kind)


def setup_inputs(seed: int = 0) -> dict:
    key_list = jax.random.split(jax.random.key(seed), 5)
    queries = draw_queries(jax.random.fold_in(key_list[4], 71), 0)
    keys = draw_keys(jax.random.fold_in(key_list[4], 71), 0)
    values = normal_values(key_list[2], (2, BLOCKS // 2, BLOCK, KV_HEADS * HEAD_DIM), 1.0, 6.0, ((1, 16), (2, 2)))
    gain = jnp.clip(1.0 + 0.18 * jax.random.normal(key_list[3], (HEAD_DIM,), jnp.float32), 0.1, 1.9)
    return dict(queries=queries, keys=keys, values=values, gain=gain)


def to_sequence(arranged):
    return jnp.concatenate([arranged[0], arranged[1][::-1]], axis=0)

def to_layout(blocked):
    half_count = BLOCKS // 2
    return jnp.stack([blocked[:half_count], blocked[half_count:][::-1]], axis=0)

def reference(queries, keys, values, gain):
    query_blocks = to_sequence(queries).reshape(BLOCKS, BLOCK, KV_HEADS, GROUP, HEAD_DIM)
    key_all = to_sequence(keys).reshape(SEQ_LEN, KV_HEADS, HEAD_DIM).astype(jnp.float32)
    value_all = to_sequence(values).reshape(SEQ_LEN, KV_HEADS, HEAD_DIM).astype(jnp.float32)
    key_block_ids = jnp.arange(SEQ_LEN, dtype=jnp.int32) // BLOCK
    scale_factor = 1.0 / math.sqrt(HEAD_DIM)
    gain_f = gain.astype(jnp.float32)

    def one_block(operands):
        query_block, block_index = operands
        scores = jnp.einsum('qgjd,kgd->qgjk', query_block.astype(jnp.float32), key_all)
        scores = scores * scale_factor
        visible = key_block_ids <= block_index
        scores = jnp.where(visible, scores, -jnp.inf)
        largest = lax.optimization_barrier(jnp.max(scores, axis=-1, keepdims=True))
        raw_weights = jnp.exp(scores - largest)
        totals = lax.optimization_barrier(jnp.sum(raw_weights, axis=-1))
        weights = lax.optimization_barrier(raw_weights.astype(jnp.bfloat16))
        mixed = jnp.einsum('qgjk,kgd->qgjd', weights.astype(jnp.float32), value_all) / totals[..., None]
        spread = jnp.sqrt(lax.optimization_barrier(jnp.mean(mixed * mixed, axis=-1, keepdims=True)) + 1e-06)
        return (mixed / spread * gain_f).astype(jnp.bfloat16)
    produced = lax.map(one_block, (query_blocks, jnp.arange(BLOCKS, dtype=jnp.int32)))
    return to_layout(produced.reshape(BLOCKS, BLOCK, HEADS * HEAD_DIM))
```

```python
import functools
import math

import jax
import jax.numpy as jnp
from jax import lax
from jax.experimental import pallas as pl
from jax.experimental.pallas import tpu as pltpu
from jax.sharding import PartitionSpec as P

KV_HEADS = 4
GROUP = 6
HEAD_DIM = 128
LOWEST = -1e30
EXPONENT = math.log2(math.e) / math.sqrt(HEAD_DIM)

DOWN, UP, ACROSS_X, ACROSS_Y, CORE = range(5)


def kernel(planes, q_ref, k_ref, v_ref, gain_ref, out_ref, qs, buf, top, total, acc,
           local_sem, send_sem, recv_sem):
    seq = lax.axis_index("seq")
    y = lax.axis_index("row")
    z, x, c = seq // 4, (seq // 2) % 2, seq % 2
    own_group = seq // 2
    rows = q_ref.shape[2]
    other_y = 1 - y
    devices = {
        DOWN: {"seq": seq - 4},
        UP: {"seq": seq + 4},
        ACROSS_X: {"seq": seq + 2 - 4 * x},
        ACROSS_Y: {"row": other_y},
        CORE: {"seq": seq + 1 - 2 * c},
    }

    load_k = pltpu.make_async_copy(k_ref.at[:, 0], buf.at[0, :, own_group, c, y], local_sem.at[0])
    load_v = pltpu.make_async_copy(v_ref.at[:, 0], buf.at[1, :, own_group, c, y], local_sem.at[1])
    load_k.start()
    load_v.start()

    barrier = pltpu.get_barrier_semaphore()

    def greet(where):
        pl.semaphore_signal(barrier, inc=1, device_id=devices[where],
                            device_id_type=pl.DeviceIdType.MESH)

    has_down, has_up = z > 0, z < planes - 1
    pl.when(has_down)(lambda: greet(DOWN))
    pl.when(has_up)(lambda: greet(UP))
    for where in (ACROSS_X, ACROSS_Y, CORE):
        greet(where)
    pl.semaphore_wait(barrier, 3 + has_down.astype(jnp.int32) + has_up.astype(jnp.int32))

    def piece(group, core, row, half, where):
        ref = buf.at[:, half, group, core, row]
        return pltpu.make_async_remote_copy(
            src_ref=ref, dst_ref=ref,
            send_sem=send_sem.at[group, row, half, where],
            recv_sem=recv_sem.at[group, core, row, half],
            device_id=devices[where], device_id_type=pl.DeviceIdType.MESH)

    def start(copy):
        copy.start()

    def finish(copy):
        copy.wait_send()

    def arrived(group, core, row, half):
        piece(group, core, row, half, CORE).wait_recv()

    def column(plane, act, wait):
        group = 2 * plane + x

        def visit(half):
            if wait:
                arrived(group, c, y, half)
            pl.when(has_down & (plane >= z))(lambda: act(piece(group, c, y, half, DOWN)))
            if half == 0:
                pl.when(has_up & (plane <= z))(lambda: act(piece(group, c, y, half, UP)))
            for where in (ACROSS_X, ACROSS_Y, CORE):
                act(piece(group, c, y, half, where))

        visit(0)
        pl.when(plane >= z)(lambda: visit(1))

    def sides(plane, act, wait):
        def visit(half):
            for across, group, row in ((0, 2 * plane + 1 - x, y), (1, 2 * plane + x, other_y)):
                if wait:
                    arrived(group, c, row, half)
                if across == half:
                    act(piece(group, c, row, half, ACROSS_X if across else ACROSS_Y))
                act(piece(group, c, row, half, CORE))

        visit(0)
        pl.when(plane >= z)(lambda: visit(1))

    def corner(plane, act, wait):
        group = 2 * plane + 1 - x

        def visit(half):
            if wait:
                arrived(group, c, other_y, half)
            act(piece(group, c, other_y, half, CORE))

        visit(0)
        pl.when(plane >= z)(lambda: visit(1))

    def from_core(plane):
        def visit(half):
            for dx in range(2):
                for dy in range(2):
                    arrived(2 * plane + dx, 1 - c, dy, half)

        visit(0)
        pl.when(plane >= z)(lambda: visit(1))

    def attend(query_half, kv_refs):
        for head in range(KV_HEADS):
            lanes = slice(head * HEAD_DIM, (head + 1) * HEAD_DIM)
            key = kv_refs[0][..., lanes].reshape(-1, HEAD_DIM)
            value = kv_refs[1][..., lanes].reshape(-1, HEAD_DIM)
            scores = lax.dot_general(key, qs[query_half, head], (((1,), (1,)), ((), ())),
                                     preferred_element_type=jnp.float32)
            old = top[query_half, head]
            new = jnp.maximum(old, jnp.max(scores, axis=0, keepdims=True))
            weights = jnp.exp2((scores - new) * EXPONENT)
            factor = jnp.exp2((old - new) * EXPONENT)
            top[query_half, head] = new
            total[query_half, head] = total[query_half, head] * factor + jnp.sum(
                weights, axis=0, keepdims=True)
            acc[query_half, head] = acc[query_half, head] * factor + lax.dot_general(
                value.T, weights.astype(jnp.bfloat16), (((1,), (0,)), ((), ())),
                preferred_element_type=jnp.float32)

    def attend_plane(plane):
        @pl.loop(0, 4)
        def _(i):
            group = 2 * plane + i // 2
            second = i % 2
            above = (group > own_group).astype(jnp.int32)
            query_half = 1 - second * (1 - above)
            key_half = second * above

            @pl.when((second == 0) | (group != own_group))
            def _():
                attend(query_half, (buf.at[0, key_half, group], buf.at[1, key_half, group]))

    def attend_own():
        @pl.loop(0, 3)
        def _(i):
            last = i // 2
            core = c + last * (1 - 2 * c)
            half = (i % 2) * (1 - last) + last * (1 - c)
            attend(half, (buf.at[0, half, own_group, core], buf.at[1, half, own_group, core]))

    load_k.wait()
    load_v.wait()
    column(z, start, False)

    for half in range(2):
        for head in range(KV_HEADS * GROUP):
            at = (head % GROUP) * rows
            qs[half, head // GROUP, at:at + rows, :] = q_ref[
                half, 0, :, head * HEAD_DIM:(head + 1) * HEAD_DIM]
    top[...] = jnp.full(top.shape, LOWEST, jnp.float32)
    total[...] = jnp.zeros(total.shape, jnp.float32)
    acc[...] = jnp.zeros(acc.shape, jnp.float32)

    @pl.loop(0, planes)
    def _(step):
        @pl.loop(0, 2)
        def _(way):
            plane = z + (step + 1) * (1 - 2 * way)

            @pl.when((plane >= 0) & (plane < planes))
            def _():
                column(plane, start, True)

        @pl.loop(0, 2)
        def _(way):
            plane = z + step * (1 - 2 * way)

            @pl.when((plane >= 0) & (plane < planes) & ((way == 0) | (step > 0)))
            def _():
                sides(plane, start, True)
                corner(plane, start, True)
                from_core(plane)
                pl.when(step == 0)(attend_own)
                attend_plane(plane)

    for half in range(2):
        for kv_head in range(KV_HEADS):
            mixed = acc[half, kv_head] / total[half, kv_head]
            spread = jnp.sqrt(jnp.mean(mixed * mixed, axis=0, keepdims=True) + 1e-06)
            normed = (mixed / spread * gain_ref[...]).T.astype(jnp.bfloat16)
            for member in range(GROUP):
                head = kv_head * GROUP + member
                out_ref[half, 0, :, head * HEAD_DIM:(head + 1) * HEAD_DIM] = normed[
                    member * rows:(member + 1) * rows]

    @pl.loop(0, planes)
    def _(plane):
        column(plane, finish, False)
        sides(plane, finish, False)
        corner(plane, finish, False)


def per_device(queries, keys, values, gain):
    seq_size = lax.axis_size("seq")
    planes = seq_size // 4
    rows, width = keys.shape[2], keys.shape[3]
    stacked = GROUP * rows
    buf_shape = (2, 2, 2 * planes, 2, 2, rows, width)
    buf_bytes = 2 * math.prod(buf_shape)
    vmem = pl.BlockSpec(memory_space=pltpu.VMEM)
    units = 2 * (2 * seq_size + 1) * rows * 2 * rows
    return pl.pallas_call(
        functools.partial(kernel, planes),
        out_shape=jax.ShapeDtypeStruct(queries.shape, jnp.bfloat16),
        in_specs=[vmem, pl.BlockSpec(memory_space=pl.ANY), pl.BlockSpec(memory_space=pl.ANY), vmem],
        out_specs=vmem,
        scratch_shapes=[
            pltpu.VMEM((2, KV_HEADS, stacked, HEAD_DIM), jnp.bfloat16),
            pltpu.VMEM(buf_shape, jnp.bfloat16),
            pltpu.VMEM((2, KV_HEADS, 1, stacked), jnp.float32),
            pltpu.VMEM((2, KV_HEADS, 1, stacked), jnp.float32),
            pltpu.VMEM((2, KV_HEADS, HEAD_DIM, stacked), jnp.float32),
            pltpu.SemaphoreType.DMA((2,)),
            pltpu.SemaphoreType.DMA((2 * planes, 2, 2, 5)),
            pltpu.SemaphoreType.DMA((2 * planes, 2, 2, 2)),
        ],
        compiler_params=pltpu.CompilerParams(
            collective_id=0, has_side_effects=True, vmem_limit_bytes=buf_bytes + 14 * 2**20
        ),
        cost_estimate=pl.CostEstimate(
            flops=units * KV_HEADS * GROUP * HEAD_DIM * 2,
            bytes_accessed=2 * queries.size * 2,
            transcendentals=units * KV_HEADS * GROUP // 2),
    )(queries, keys, values, gain.reshape(HEAD_DIM, 1))


def solution(mesh):
    return jax.shard_map(
        per_device,
        mesh=mesh,
        in_specs=(
            P(None, "seq", "row", None),
            P(None, "seq", "row", None),
            P(None, "seq", "row", None),
            P(),
        ),
        out_specs=P(None, "seq", "row", None),
        check_vma=False,
    )
```

```python
import functools
import math

import jax
import jax.numpy as jnp
from jax import lax
from jax.experimental import pallas as pl
from jax.experimental.pallas import tpu as pltpu
from jax.sharding import PartitionSpec as P

KV_HEADS = 4
GROUP = 6
HEAD_DIM = 128
LOWEST = -1e30
EXPONENT = math.log2(math.e) / math.sqrt(HEAD_DIM)

DOWN, UP, ACROSS_X, ACROSS_Y, CORE = range(5)


def kernel(planes, q_hbm, k_ref, v_ref, gain_ref, out_ref, q_ref, qs, buf, top, total, acc,
           local_sem, send_sem, recv_sem):
    seq = lax.axis_index("seq")
    y = lax.axis_index("row")
    z, x, c = seq // 4, (seq // 2) % 2, seq % 2
    own_group = seq // 2
    rows = q_ref.shape[2]
    other_y = 1 - y
    devices = {
        DOWN: {"seq": seq - 4},
        UP: {"seq": seq + 4},
        ACROSS_X: {"seq": seq + 2 - 4 * x},
        ACROSS_Y: {"row": other_y},
        CORE: {"seq": seq + 1 - 2 * c},
    }

    load_k = pltpu.make_async_copy(k_ref.at[:, 0], buf.at[0, :, own_group, c, y], local_sem.at[0])
    load_v = pltpu.make_async_copy(v_ref.at[:, 0], buf.at[1, :, own_group, c, y], local_sem.at[1])
    load_k.start()
    load_v.start()
    load_q = pltpu.make_async_copy(q_hbm, q_ref, local_sem.at[2])
    load_q.start()

    barrier = pltpu.get_barrier_semaphore()

    def greet(where):
        pl.semaphore_signal(barrier, inc=1, device_id=devices[where],
                            device_id_type=pl.DeviceIdType.MESH)

    has_down, has_up = z > 0, z < planes - 1
    pl.when(has_down)(lambda: greet(DOWN))
    pl.when(has_up)(lambda: greet(UP))
    for where in (ACROSS_X, ACROSS_Y, CORE):
        greet(where)
    pl.semaphore_wait(barrier, 3 + has_down.astype(jnp.int32) + has_up.astype(jnp.int32))

    def piece(group, core, row, half, where):
        ref = buf.at[:, half, group, core, row]
        return pltpu.make_async_remote_copy(
            src_ref=ref, dst_ref=ref,
            send_sem=send_sem.at[group, row, half, where],
            recv_sem=recv_sem.at[group, core, row, half],
            device_id=devices[where], device_id_type=pl.DeviceIdType.MESH)

    def start(copy):
        copy.start()

    def finish(copy):
        copy.wait_send()

    def arrived(group, core, row, half):
        piece(group, core, row, half, CORE).wait_recv()

    def column(plane, act, wait):
        group = 2 * plane + x

        def visit(half):
            if wait:
                arrived(group, c, y, half)
            pl.when(has_down & (plane >= z))(lambda: act(piece(group, c, y, half, DOWN)))
            if half == 0:
                pl.when(has_up & (plane <= z))(lambda: act(piece(group, c, y, half, UP)))
            for where in (ACROSS_X, ACROSS_Y, CORE):
                act(piece(group, c, y, half, where))

        visit(0)
        pl.when(plane >= z)(lambda: visit(1))

    def sides(plane, act, wait):
        def visit(half):
            for across, group, row in ((0, 2 * plane + 1 - x, y), (1, 2 * plane + x, other_y)):
                if wait:
                    arrived(group, c, row, half)
                if across == half:
                    act(piece(group, c, row, half, ACROSS_X if across else ACROSS_Y))
                act(piece(group, c, row, half, CORE))

        visit(0)
        pl.when(plane >= z)(lambda: visit(1))

    def corner(plane, act, wait):
        group = 2 * plane + 1 - x

        def visit(half):
            if wait:
                arrived(group, c, other_y, half)
            act(piece(group, c, other_y, half, CORE))

        visit(0)
        pl.when(plane >= z)(lambda: visit(1))

    def from_core(plane):
        def visit(half):
            for dx in range(2):
                for dy in range(2):
                    arrived(2 * plane + dx, 1 - c, dy, half)

        visit(0)
        pl.when(plane >= z)(lambda: visit(1))

    def attend(query_half, kv_refs):
        heads = range(KV_HEADS)
        cut = [slice(h * HEAD_DIM, (h + 1) * HEAD_DIM) for h in heads]
        old = [top[query_half, h] for h in heads]
        old_total = [total[query_half, h] for h in heads]
        scores = [lax.dot_general(kv_refs[0][..., cut[h]].reshape(-1, HEAD_DIM), qs[query_half, h],
                                  (((1,), (1,)), ((), ())),
                                  preferred_element_type=jnp.float32) for h in heads]
        new = [jnp.maximum(old[h], jnp.max(scores[h], axis=0, keepdims=True)) for h in heads]
        weights = [jnp.exp2((scores[h] - new[h]) * EXPONENT) for h in heads]
        factor = [jnp.exp2((old[h] - new[h]) * EXPONENT) for h in heads]
        added = [jnp.sum(weights[h], axis=0, keepdims=True) for h in heads]
        mixed = [lax.dot_general(
            kv_refs[1][..., cut[h]].reshape(-1, HEAD_DIM).T, weights[h].astype(jnp.bfloat16),
            (((1,), (0,)), ((), ())), preferred_element_type=jnp.float32) for h in heads]
        old_acc = [acc[query_half, h] for h in heads]
        for h in heads:
            top[query_half, h] = new[h]
            total[query_half, h] = old_total[h] * factor[h] + added[h]
            acc[query_half, h] = old_acc[h] * factor[h] + mixed[h]

    def attend_plane(plane):
        @pl.loop(0, 4)
        def _(i):
            group = 2 * plane + i // 2
            second = i % 2
            above = (group > own_group).astype(jnp.int32)
            query_half = 1 - second * (1 - above)
            key_half = second * above

            @pl.when((second == 0) | (group != own_group))
            def _():
                attend(query_half, (buf.at[0, key_half, group], buf.at[1, key_half, group]))

    def attend_own():
        @pl.loop(0, 3)
        def _(i):
            last = i // 2
            core = c + last * (1 - 2 * c)
            half = (i % 2) * (1 - last) + last * (1 - c)
            attend(half, (buf.at[0, half, own_group, core], buf.at[1, half, own_group, core]))

    load_k.wait()
    load_v.wait()
    column(z, start, False)
    load_q.wait()

    for half in range(2):
        for head in range(KV_HEADS * GROUP):
            at = (head % GROUP) * rows
            qs[half, head // GROUP, at:at + rows, :] = q_ref[
                half, 0, :, head * HEAD_DIM:(head + 1) * HEAD_DIM]
    top[...] = jnp.full(top.shape, LOWEST, jnp.float32)
    total[...] = jnp.zeros(total.shape, jnp.float32)
    acc[...] = jnp.zeros(acc.shape, jnp.float32)

    def at_distance(distance, visit):
        @pl.when((distance >= 0) & (distance < planes))
        def _():
            @pl.loop(0, 2)
            def _(way):
                plane = z + distance * (1 - 2 * way)
                pl.when((plane >= 0) & (plane < planes) & ((way == 0) | (distance > 0)))(
                    lambda: visit(plane))

    def pass_on_column(plane):
        pl.when(plane != z)(lambda: column(plane, start, True))

    def take_rest(plane):
        corner(plane, start, True)
        from_core(plane)

    def compute(plane):
        pl.when(plane == z)(attend_own)
        attend_plane(plane)

    @pl.loop(0, planes + 2)
    def _(step):
        at_distance(step, pass_on_column)
        at_distance(step - 1, lambda plane: sides(plane, start, True))
        at_distance(step - 2, take_rest)
        at_distance(step - 2, compute)

    for half in range(2):
        for kv_head in range(KV_HEADS):
            mixed = acc[half, kv_head] / total[half, kv_head]
            spread = jnp.sqrt(jnp.mean(mixed * mixed, axis=0, keepdims=True) + 1e-06)
            normed = ((mixed / spread).T * gain_ref[...]).astype(jnp.bfloat16)
            for member in range(GROUP):
                head = kv_head * GROUP + member
                out_ref[half, 0, :, head * HEAD_DIM:(head + 1) * HEAD_DIM] = normed[
                    member * rows:(member + 1) * rows]

    @pl.loop(0, planes)
    def _(plane):
        column(plane, finish, False)
        sides(plane, finish, False)
        corner(plane, finish, False)


def per_device(queries, keys, values, gain):
    seq_size = lax.axis_size("seq")
    planes = seq_size // 4
    rows, width = keys.shape[2], keys.shape[3]
    stacked = GROUP * rows
    buf_shape = (2, 2, 2 * planes, 2, 2, rows, width)
    vmem = pl.BlockSpec(memory_space=pltpu.VMEM)
    units = 2 * (2 * seq_size + 1) * rows * 2 * rows
    return pl.pallas_call(
        functools.partial(kernel, planes),
        out_shape=jax.ShapeDtypeStruct(queries.shape, jnp.bfloat16),
        in_specs=[pl.BlockSpec(memory_space=pltpu.HBM)] * 3 + [vmem],
        out_specs=vmem,
        scratch_shapes=[
            pltpu.VMEM(queries.shape, jnp.bfloat16),
            pltpu.VMEM((2, KV_HEADS, stacked, HEAD_DIM), jnp.bfloat16),
            pltpu.VMEM(buf_shape, jnp.bfloat16),
            pltpu.VMEM((2, KV_HEADS, 1, stacked), jnp.float32),
            pltpu.VMEM((2, KV_HEADS, 1, stacked), jnp.float32),
            pltpu.VMEM((2, KV_HEADS, HEAD_DIM, stacked), jnp.float32),
            pltpu.SemaphoreType.DMA((3,)),
            pltpu.SemaphoreType.DMA((2 * planes, 2, 2, 5)),
            pltpu.SemaphoreType.DMA((2 * planes, 2, 2, 2)),
        ],
        compiler_params=pltpu.CompilerParams(
            collective_id=0, has_side_effects=True, vmem_limit_bytes=56 * 2**20
        ),
        cost_estimate=pl.CostEstimate(
            flops=units * KV_HEADS * GROUP * HEAD_DIM * 2,
            bytes_accessed=2 * queries.size * 2,
            transcendentals=units * KV_HEADS * GROUP // 2),
    )(queries, keys, values, gain.reshape(1, HEAD_DIM))


def solution(mesh):
    return jax.shard_map(
        per_device,
        mesh=mesh,
        in_specs=(
            P(None, "seq", "row", None),
            P(None, "seq", "row", None),
            P(None, "seq", "row", None),
            P(),
        ),
        out_specs=P(None, "seq", "row", None),
        check_vma=False,
    )
```

```python
import functools
import math

import jax
import jax.numpy as jnp
from jax import lax
from jax.experimental import pallas as pl
from jax.experimental.pallas import tpu as pltpu
from jax.sharding import PartitionSpec as P

KV_HEADS = 4
GROUP = 6
HEAD_DIM = 128
LOWEST = -1e30
EXPONENT = math.log2(math.e) / math.sqrt(HEAD_DIM)

KV_HERE = KV_HEADS // 2
KV_WIDTH = KV_HERE * HEAD_DIM
HEAD_WIDTH = GROUP * HEAD_DIM
Q_WIDTH = KV_HERE * HEAD_WIDTH

DOWN, UP, ACROSS_X, CORE = range(4)
MESH = pl.DeviceIdType.MESH


def kernel(planes, q_ref, k_ref, v_ref, gain_ref, out_ref, q_all, qs, buf, top, total, acc, made,
           local_sem, swap_send, swap_recv, keep_sem, back_send, back_recv, send_sem, recv_sem):
    seq = lax.axis_index("seq")
    y = lax.axis_index("row")
    z, x, c = seq // 4, (seq // 2) % 2, seq % 2
    own_group = seq // 2
    rows = q_all.shape[2]
    other_y = 1 - y
    devices = {
        DOWN: {"seq": seq - 4},
        UP: {"seq": seq + 4},
        ACROSS_X: {"seq": seq + 2 - 4 * x},
        CORE: {"seq": seq + 1 - 2 * c},
    }
    partner = {"row": other_y}

    def columns(which, width):
        return pl.ds(pl.multiple_of(which * width, width), width)

    sources = ((k_ref, buf.at[0, :, own_group, c, y], KV_WIDTH),
               (v_ref, buf.at[1, :, own_group, c, y], KV_WIDTH),
               (q_ref, q_all.at[:, y], Q_WIDTH))
    loads = [pltpu.make_async_copy(ref.at[:, 0, :, columns(y, width)], to, local_sem.at[i])
             for i, (ref, to, width) in enumerate(sources)]
    swaps = [pltpu.make_async_remote_copy(
        src_ref=ref.at[:, 0, :, columns(other_y, width)], dst_ref=to,
        send_sem=swap_send.at[i], recv_sem=swap_recv.at[i],
        device_id=partner, device_id_type=MESH) for i, (ref, to, width) in enumerate(sources)]
    for load in loads:
        load.start()

    barrier = pltpu.get_barrier_semaphore()

    def greet(device):
        pl.semaphore_signal(barrier, inc=1, device_id=device, device_id_type=MESH)

    has_down, has_up = z > 0, z < planes - 1
    pl.when(has_down)(lambda: greet(devices[DOWN]))
    pl.when(has_up)(lambda: greet(devices[UP]))
    for device in (devices[ACROSS_X], devices[CORE], partner):
        greet(device)
    pl.semaphore_wait(barrier, 3 + has_down.astype(jnp.int32) + has_up.astype(jnp.int32))

    def piece(group, core, row, half, where):
        ref = buf.at[:, half, group, core, row]
        return pltpu.make_async_remote_copy(
            src_ref=ref, dst_ref=ref,
            send_sem=send_sem.at[group, row, half, where],
            recv_sem=recv_sem.at[group, core, row, half],
            device_id=devices[where], device_id_type=MESH)

    def start(copy):
        copy.start()

    def finish(copy):
        copy.wait_send()

    def arrived(group, core, row, half):
        piece(group, core, row, half, CORE).wait_recv()

    def column_row(plane, row, act, wait):
        group = 2 * plane + x

        def visit(half):
            if wait:
                arrived(group, c, row, half)
            pl.when(has_down & (plane >= z))(lambda: act(piece(group, c, row, half, DOWN)))
            if half == 0:
                pl.when(has_up & (plane <= z))(lambda: act(piece(group, c, row, half, UP)))
            act(piece(group, c, row, half, ACROSS_X))
            act(piece(group, c, row, half, CORE))

        visit(0)
        pl.when(plane >= z)(lambda: visit(1))

    def column(plane, act, wait):
        column_row(plane, y, act, wait)
        column_row(plane, other_y, act, wait)

    def side(plane, act, wait):
        group = 2 * plane + 1 - x

        def visit(half):
            for row in (y, other_y):
                if wait:
                    arrived(group, c, row, half)
                act(piece(group, c, row, half, CORE))

        visit(0)
        pl.when(plane >= z)(lambda: visit(1))

    def from_core(plane):
        def visit(half):
            for dx in range(2):
                for dy in range(2):
                    arrived(2 * plane + dx, 1 - c, dy, half)

        visit(0)
        pl.when(plane >= z)(lambda: visit(1))

    def attend(query_half, kv_refs):
        heads = range(KV_HERE)
        cut = [slice(h * HEAD_DIM, (h + 1) * HEAD_DIM) for h in heads]
        old = [top[query_half, h] for h in heads]
        old_total = [total[query_half, h] for h in heads]
        scores = [lax.dot_general(kv_refs[0][..., cut[h]].reshape(-1, HEAD_DIM), qs[query_half, h],
                                  (((1,), (1,)), ((), ())),
                                  preferred_element_type=jnp.float32) for h in heads]
        new = [jnp.maximum(old[h], jnp.max(scores[h], axis=0, keepdims=True)) for h in heads]
        weights = [jnp.exp2((scores[h] - new[h]) * EXPONENT) for h in heads]
        factor = [jnp.exp2((old[h] - new[h]) * EXPONENT) for h in heads]
        added = [jnp.sum(weights[h], axis=0, keepdims=True) for h in heads]
        mixed = [lax.dot_general(
            kv_refs[1][..., cut[h]].reshape(-1, HEAD_DIM).T, weights[h].astype(jnp.bfloat16),
            (((1,), (0,)), ((), ())), preferred_element_type=jnp.float32) for h in heads]
        old_acc = [acc[query_half, h] for h in heads]
        for h in heads:
            top[query_half, h] = new[h]
            total[query_half, h] = old_total[h] * factor[h] + added[h]
            acc[query_half, h] = old_acc[h] * factor[h] + mixed[h]

    def attend_plane(plane):
        @pl.loop(0, 4)
        def _(i):
            group = 2 * plane + i // 2
            second = i % 2
            above = (group > own_group).astype(jnp.int32)
            query_half = 1 - second * (1 - above)
            key_half = second * above

            @pl.when((second == 0) | (group != own_group))
            def _():
                attend(query_half, (buf.at[0, key_half, group], buf.at[1, key_half, group]))

    def attend_own():
        @pl.loop(0, 3)
        def _(i):
            last = i // 2
            core = c + last * (1 - 2 * c)
            half = (i % 2) * (1 - last) + last * (1 - c)
            attend(half, (buf.at[0, half, own_group, core], buf.at[1, half, own_group, core]))

    def result_copies(half, kv_head):
        here = pl.ds(kv_head * HEAD_WIDTH, HEAD_WIDTH)
        there = out_ref.at[half, 0, :, columns(y * KV_HERE + kv_head, HEAD_WIDTH)]
        keep = pltpu.make_async_copy(made.at[half, y, :, here], there, keep_sem.at[half, kv_head])
        back = pltpu.make_async_remote_copy(
            src_ref=made.at[half, other_y, :, here], dst_ref=there,
            send_sem=back_send.at[half, kv_head], recv_sem=back_recv.at[half, kv_head],
            device_id=partner, device_id_type=MESH)
        return keep, back

    def emit(half):
        for kv_head in range(KV_HERE):
            mixed = acc[half, kv_head] / total[half, kv_head]
            spread = jnp.sqrt(jnp.mean(mixed * mixed, axis=0, keepdims=True) + 1e-06)
            normed = ((mixed / spread).T * gain_ref[...]).astype(jnp.bfloat16)
            for member in range(GROUP):
                lane = (kv_head * GROUP + member) * HEAD_DIM
                for row in range(2):
                    at = (2 * member + row) * rows
                    made[half, row, :, lane:lane + HEAD_DIM] = normed[at:at + rows]
            keep, back = result_copies(half, kv_head)
            back.start()
            keep.start()

    swaps[0].start()
    swaps[1].start()
    loads[0].wait()
    loads[1].wait()
    column_row(z, y, start, False)
    top[...] = jnp.full(top.shape, LOWEST, jnp.float32)
    total[...] = jnp.zeros(total.shape, jnp.float32)
    acc[...] = jnp.zeros(acc.shape, jnp.float32)
    swaps[0].wait_recv()
    swaps[1].wait_recv()
    column_row(z, other_y, start, False)
    swaps[2].start()

    def at_distance(distance, visit):
        @pl.when((distance >= 0) & (distance < planes))
        def _():
            @pl.loop(0, 2)
            def _(way):
                plane = z + distance * (1 - 2 * way)
                pl.when((plane >= 0) & (plane < planes) & ((way == 0) | (distance > 0)))(
                    lambda: visit(plane))

    def take_queries():
        loads[2].wait()
        swaps[2].wait_recv()
        for half in range(2):
            for head in range(KV_HERE * GROUP):
                for row in range(2):
                    at = (2 * (head % GROUP) + row) * rows
                    qs[half, head // GROUP, at:at + rows, :] = q_all[
                        half, row, :, head * HEAD_DIM:(head + 1) * HEAD_DIM]

    def pass_on_column(plane):
        pl.when(plane != z)(lambda: column(plane, start, True))

    def compute(plane):
        from_core(plane)

        @pl.when(plane == z)
        def _():
            take_queries()
            attend_own()

        attend_plane(plane)

    @pl.loop(0, planes + 2)
    def _(step):
        at_distance(step, pass_on_column)
        at_distance(step - 2, compute)
        pl.when(step - 2 == z)(lambda: emit(0))
        at_distance(step - 1, lambda plane: side(plane, start, True))

    emit(1)

    @pl.loop(0, planes)
    def _(plane):
        column(plane, finish, False)
        side(plane, finish, False)

    for swap in swaps:
        swap.wait_send()
    for half in range(2):
        for kv_head in range(KV_HERE):
            keep, back = result_copies(half, kv_head)
            keep.wait()
            back.wait()


def per_device(queries, keys, values, gain):
    seq_size = lax.axis_size("seq")
    planes = seq_size // 4
    rows = keys.shape[2]
    stacked = GROUP * 2 * rows
    hbm = pl.BlockSpec(memory_space=pltpu.HBM)
    units = 2 * (2 * seq_size + 1) * rows * 2 * rows
    return pl.pallas_call(
        functools.partial(kernel, planes),
        out_shape=jax.ShapeDtypeStruct(queries.shape, jnp.bfloat16),
        in_specs=[hbm, hbm, hbm, pl.BlockSpec(memory_space=pltpu.VMEM)],
        out_specs=hbm,
        scratch_shapes=[
            pltpu.VMEM((2, 2, rows, Q_WIDTH), jnp.bfloat16),
            pltpu.VMEM((2, KV_HERE, stacked, HEAD_DIM), jnp.bfloat16),
            pltpu.VMEM((2, 2, 2 * planes, 2, 2, rows, KV_WIDTH), jnp.bfloat16),
            pltpu.VMEM((2, KV_HERE, 1, stacked), jnp.float32),
            pltpu.VMEM((2, KV_HERE, 1, stacked), jnp.float32),
            pltpu.VMEM((2, KV_HERE, HEAD_DIM, stacked), jnp.float32),
            pltpu.VMEM((2, 2, rows, Q_WIDTH), jnp.bfloat16),
            pltpu.SemaphoreType.DMA((3,)),
            pltpu.SemaphoreType.DMA((3,)),
            pltpu.SemaphoreType.DMA((3,)),
            pltpu.SemaphoreType.DMA((2, KV_HERE)),
            pltpu.SemaphoreType.DMA((2, KV_HERE)),
            pltpu.SemaphoreType.DMA((2, KV_HERE)),
            pltpu.SemaphoreType.DMA((2 * planes, 2, 2, 4)),
            pltpu.SemaphoreType.DMA((2 * planes, 2, 2, 2)),
        ],
        compiler_params=pltpu.CompilerParams(
            collective_id=0, has_side_effects=True, vmem_limit_bytes=56 * 2**20
        ),
        cost_estimate=pl.CostEstimate(
            flops=units * KV_HEADS * GROUP * HEAD_DIM * 2,
            bytes_accessed=2 * queries.size * 2,
            transcendentals=units * KV_HEADS * GROUP // 2),
    )(queries, keys, values, gain.reshape(1, HEAD_DIM))


def solution(mesh):
    return jax.shard_map(
        per_device,
        mesh=mesh,
        in_specs=(
            P(None, "seq", "row", None),
            P(None, "seq", "row", None),
            P(None, "seq", "row", None),
            P(),
        ),
        out_specs=P(None, "seq", "row", None),
        check_vma=False,
    )
```
